1024 devices in a mesh: expert: 16 (over y, x_lo, core), dp: 64 (over x_hi, z).
Axes of the slice: x: 4 (x_hi: 2, x_lo: 2; x = x_hi * 2 + x_lo), y: 4, z: 32, core: 2. Of those that a mesh axis runs over, the one named last changes fastest.
Arguments:
- tokens: bfloat16 [8192, 2048], P('dp'), may hold values from -6 to 6
- cotangent: bfloat16 [8192, 2048], P('dp'), may hold values from -6 to 6
- gate_values: float32 [8192, 2], P('dp'), may hold values from 0.2 to 1
- expert_ids: int32 [8192, 2], P('dp'), may hold values from 0 to 63, all different within a row
- weight_in: bfloat16 [64, 2048, 4096], P('dp', None, 'expert'), may hold values from -0.125 to 0.125
- weight_out: bfloat16 [64, 4096, 2048], P('dp', 'expert'), may hold values from -0.09375 to 0.09375
Outputs:
- input_grad: bfloat16 [8192, 2048], P('dp', 'expert')
- weight_out_grad: bfloat16 [64, 4096, 2048], P('dp', 'expert')
The draws below stay inside these ranges and needn't reach their ends.
All inputs are finite; a program needn't handle non-finite values.
Results may differ from the reference program's by a relative error of at most 0.0057.
Values may be sent and summed in bfloat16 or wider, within the bound.
A program may use at most 32 MiB of HBM per device.

```python
import jax
import jax.numpy as jnp
from jax import lax

D = 2048
FF = 4096
CAP = 4
TOK_DEV = 128
EXPERTS = 64
TOKENS = 8192
N_DP = 64


def block_levels(stream_key, extent, shards, low, largest):
    factor_of = 1.0
    for dim, blocks in shards:
        draws = jax.random.uniform(jax.random.fold_in(jax.random.fold_in(stream_key, 6), dim), (blocks,), jnp.float32, low / len(shards), largest / len(shards))
        factor_of = factor_of * jnp.repeat(jnp.exp(draws), extent[dim] // blocks).reshape((-1,) + (1,) * (len(extent) - 1 - dim))
    return factor_of


def distinct(rng, rows, count, top, lift):
    order = jax.random.permutation(jax.random.fold_in(rng, 1), count)
    pull = order
    for power in range(3):
        pull = pull * pull // count
    pull = pull * lift // count
    tickets = jax.random.randint(jax.random.fold_in(rng, 2), (rows, count), 0, 4096) + pull
    sure = jax.random.permutation(jax.random.fold_in(rng, 3), rows)[jnp.arange(count) % rows]
    tickets = jnp.where(jnp.arange(rows)[:, None] == sure[None, :], 1 << 14, tickets)
    priority = tickets * count + jnp.arange(count)
    return lax.top_k(priority.astype(jnp.int32), top)[1].astype(jnp.int32)


def normal_values(own_key, dims, deviation, bound, shards=(), kind=jnp.bfloat16):
    level = block_levels(own_key, dims, shards, -0.22, 0.18) if shards else 1.0
    array = jax.random.normal(own_key, dims, jnp.float32) * deviation * level
    return jnp.minimum(jnp.maximum(array, -bound), bound).astype(kind)


def setup_inputs(seed: int = 0) -> dict:
    arg_keys = jax.random.split(jax.random.key(seed), 7)
    tokens = normal_values(arg_keys[0], (TOKENS, D), 1.0, 6.0, ((0, 64),))
    cotangent = normal_values(arg_keys[1], (TOKENS, D), 1.0, 6.0, ((0, 64),))
    gate_values = jnp.clip(0.2 + 0.8 * jax.random.uniform(arg_keys[2], (TOKENS, 2), jnp.float32) ** block_levels(arg_keys[2], (TOKENS, 2), ((0, 64),), -0.2, 0.2), 0.2, 1.0)
    expert_ids = distinct(arg_keys[3], TOKENS, EXPERTS, 2, 512)
    weight_in = normal_values(arg_keys[4], (EXPERTS, D, FF), D ** -0.5, 0.125, ((0, 64), (2, 16)))
    weight_out = normal_values(arg_keys[5], (EXPERTS, FF, D), FF ** -0.5, 0.09375, ((0, 64), (1, 16)))
    return {"tokens": tokens, "cotangent": cotangent, "gate_values": gate_values, "expert_ids": expert_ids, "weight_in": weight_in, "weight_out": weight_out}


def reference(tokens, cotangent, gate_values, expert_ids, weight_in, weight_out):
    groups = N_DP
    per_group = TOK_DEV
    expert_count = EXPERTS
    grouped_ids = expert_ids.reshape(groups, per_group * 2)
    onehot = (grouped_ids[:, :, None] == jnp.arange(expert_count, dtype=jnp.int32)[None, None, :]).astype(jnp.int32)
    before = jnp.cumsum(onehot, axis=1) - onehot
    position = lax.optimization_barrier(jnp.sum(before * onehot, axis=2))
    target = jnp.where(position < CAP, grouped_ids * CAP + position, -1).reshape(groups, per_group, 2)
    slot_table = target[..., None] == jnp.arange(expert_count * CAP, dtype=jnp.int32)[None, None, None, :]
    dispatch = jnp.any(slot_table, axis=2).astype(jnp.float32)
    slot_gate = lax.optimization_barrier(jnp.sum(slot_table.astype(jnp.float32) * gate_values.reshape(groups, per_group, 2)[..., None].astype(jnp.float32), axis=(1, 2)))
    token_groups = tokens.reshape(groups, per_group, D).astype(jnp.float32)
    grad_groups = cotangent.reshape(groups, per_group, D).astype(jnp.float32)
    buffer_tokens = jnp.einsum('gts,gtd->gsd', dispatch, token_groups, precision=lax.Precision.HIGHEST).astype(jnp.bfloat16)
    buffer_grads = (jnp.einsum('gts,gtd->gsd', dispatch, grad_groups, precision=lax.Precision.HIGHEST) * slot_gate[..., None]).astype(jnp.bfloat16)
    expert_rows = buffer_tokens.reshape(groups, expert_count, CAP, D).transpose(1, 0, 2, 3).reshape(expert_count, groups * CAP, D)
    expert_grads = buffer_grads.reshape(groups, expert_count, CAP, D).transpose(1, 0, 2, 3).reshape(expert_count, groups * CAP, D)

    def one_expert(operands):
        rows_x, rows_g, first_weight, second_weight = operands
        preact = jnp.dot(rows_x, first_weight, preferred_element_type=jnp.float32)
        hidden, puller = jax.vjp(jax.nn.gelu, preact)
        post_grad = jnp.dot(rows_g, second_weight.T, preferred_element_type=jnp.float32)
        pre_grad = puller(post_grad)[0].astype(jnp.bfloat16)
        out_grad = jnp.dot(hidden.astype(jnp.bfloat16).T, rows_g, preferred_element_type=jnp.float32).astype(jnp.bfloat16)
        slot_inputs = jnp.dot(pre_grad, first_weight.T, preferred_element_type=jnp.float32)
        return (out_grad, slot_inputs)
    out_grads, slot_inputs = lax.map(one_expert, (expert_rows, expert_grads, weight_in, weight_out))
    slot_inputs = slot_inputs.reshape(expert_count, groups, CAP, D).transpose(1, 0, 2, 3).reshape(groups, expert_count * CAP, D)
    input_grad = jnp.einsum('gts,gsd->gtd', dispatch, slot_inputs, precision=lax.Precision.HIGHEST)
    return (input_grad.astype(jnp.bfloat16).reshape(TOKENS, D), out_grads)
```

```python
import functools

import jax
import jax.numpy as jnp
from jax import lax
from jax.experimental import pallas as pl
from jax.experimental.pallas import tpu as pltpu
from jax.sharding import PartitionSpec as P

CAP = 4
PLANE = 16
NZ = 32
WAYS = 4
ROWS = WAYS * CAP
F32 = jnp.float32
BF16 = jnp.bfloat16
NT = (((1,), (1,)), ((), ()))
TN = (((0,), (0,)), ((), ()))
K0 = 0.7978845608028654
K1 = 0.044715


def rem(a, b):
    return lax.rem(a, b)


def iota(shape, dim):
    return lax.broadcasted_iota(jnp.int32, shape, dim)


def offsets(a):
    return (a + 1, 16 - a, 32 - a, 17 + a)


def kernel(
    tok_hbm, cot_hbm, ids_ref, gate_ref, win_hbm, wout_hbm, out_ref, wog_hbm,
    tok, cot, win, wout, wog, tx, rx, rows_all, pre_grad, hid,
    e1s, e1r, q_ref, e2s, e2r, e3s, e3r, e4s, e4r, fs, fr, ts, tr, dall,
    ld_sem, b_s, b_r, c1_s, c1_r, c2_s, c2_r, c3_s, c3_r, sib_s, sib_r,
    e1_ss, e1_rs, e2_ss, e2_rs, e3_ss, e3_rs, e4_ss, e4_rs, f_ss, f_rs, t_ss, t_rs,
):
    width = tok.shape[1]
    m = lax.axis_index("expert")
    d = lax.axis_index("dp")
    y, xl, c = m // 4, rem(m // 2, 2), rem(m, 2)
    xh, z = d // NZ, rem(d, NZ)
    a = y * 2 + xl
    p = c * 8 + a
    off = offsets(a)
    xo = rem(xh + c, 2)
    dest = [xo * NZ + rem(z + o, NZ) for o in off]
    source = [xo * NZ + rem(z + NZ - o, NZ) for o in off]
    to_self = (a == 0) & (c == 0)
    sibling = m + 1 - 2 * c
    partner = m + 2 - 4 * xl
    up = rem(y + 1, 4) * 4 + rem(m, 4)
    down = rem(y + 3, 4) * 4 + rem(m, 4)

    def plane_index(q):
        return rem(q, 8) * 2 + q // 8

    loads = [
        pltpu.make_async_copy(src, dst, ld_sem.at[i])
        for i, (src, dst) in enumerate(((tok_hbm, tok), (cot_hbm, cot), (win_hbm, win), (wout_hbm, wout)))
    ]
    for copy in loads:
        copy.start()
    barrier = pltpu.get_barrier_semaphore()

    def greet(e, dp):
        pl.semaphore_signal(barrier, inc=1, device_id={"expert": e, "dp": dp}, device_id_type=pl.DeviceIdType.MESH)

    for j in range(WAYS):
        if j == 2:
            @pl.when(jnp.logical_not(to_self))
            def _():
                greet(m, dest[2])
                greet(m, source[2])
        else:
            greet(m, dest[j])
            greet(m, source[j])
    for i in range(1, PLANE):
        greet(plane_index(rem(p + i, PLANE)), d)

    id0, id1 = ids_ref[0:1, :], ids_ref[1:2, :]
    g0, g1 = gate_ref[0:1, :], gate_ref[1:2, :]
    count = id0.shape[1]
    earlier = (iota((count, count), 0) < iota((count, count), 1)).astype(BF16)

    def slots(expert, slot):
        one0, one1 = id0 == expert, id1 == expert
        one = one0 | one1
        before = jnp.dot(one.astype(F32).astype(BF16), earlier, preferred_element_type=F32)
        taken = one & (before.astype(jnp.int32) == slot)
        return taken, one0

    r = iota((4 * ROWS, 1), 0)
    rj, rq, rs = r // 16, rem(r // 4, 4), rem(r, 4)
    expert = jnp.where(rj == 0, dest[0], jnp.where(rj == 1, dest[1], jnp.where(rj == 2, dest[2], dest[3])))
    taken, one0 = slots(expert, rs)
    gate = jnp.sum(jnp.where(taken, jnp.where(one0, g0, g1), 0.0), axis=1, keepdims=True)
    picks = [(taken & (rq == q)).astype(F32).astype(BF16) for q in range(4)]
    quarter = width // 4

    def fill(stream, ref, scale):
        total = None
        for q in range(4):
            part = jnp.dot(picks[q], ref[:, q * quarter:(q + 1) * quarter], preferred_element_type=F32)
            total = part if total is None else total + part
        if scale is not None:
            total = total * scale
        tx[stream] = total.astype(BF16)

    loads[0].wait()
    fill(0, tok, None)
    pl.semaphore_wait(barrier, 8 + PLANE - 1 - 2 * to_self.astype(jnp.int32))

    waits = []

    def remote(src, dst, send, recv, e=None, dp=None):
        return pltpu.make_async_remote_copy(
            src_ref=src, dst_ref=dst, send_sem=send, recv_sem=recv,
            device_id={"expert": m if e is None else e, "dp": d if dp is None else dp},
            device_id_type=pl.DeviceIdType.MESH,
        )

    def go(copy):
        copy.start()
        waits.append(copy)
        return copy

    def exchange(src, dst, send, recv, dp, is_self):
        copy = remote(src, dst, send, recv, dp=dp)
        if not is_self:
            return go(copy)

        @pl.when(jnp.logical_not(to_self))
        def _():
            copy.start()

        @pl.when(to_self)
        def _():
            pltpu.make_async_copy(src, dst, recv).start()

        return copy

    guarded = []

    def block(ref, j):
        return ref.at[pl.ds(j * 16, 16)]

    def send_b(stream):
        out = []
        for j in (1, 3, 0, 2):
            copy = exchange(block(tx.at[stream], j), block(rx.at[stream], j), b_s.at[stream, j], b_r.at[stream, j], dest[j], j == 2)
            out.append(copy)
            if j == 2:
                guarded.append(copy)
        return out

    b_copies = [send_b(0)]
    loads[1].wait()
    fill(1, cot, gate)
    b_copies.append(send_b(1))

    t = iota((64, 64), 0)
    u = iota((64, 64), 1)
    swap = ((t // 16 == rem(u // 4, 4)) & (rem(t // 4, 4) == u // 16) & (rem(t, 4) == rem(u, 4))).astype(F32).astype(BF16)

    ar = iota((PLANE * ROWS, 1), 0)
    ap, aj, asl = ar // 16, rem(ar // 4, 4), rem(ar, 4)
    ac, aa = ap // 8, rem(ap, 8)
    aoff = jnp.where(aj == 0, aa + 1, jnp.where(aj == 1, 16 - aa, jnp.where(aj == 2, 32 - aa, 17 + aa)))
    aexpert = rem(xh + ac, 2) * NZ + rem(z + aoff, NZ)
    all_taken, _ = slots(aexpert, asl)
    dall[...] = all_taken.astype(F32).astype(BF16)

    def unpack(stream):
        for copy in b_copies[stream]:
            copy.wait_recv()
        got = jnp.dot(swap, rx[stream], preferred_element_type=F32).astype(BF16)
        for q in range(4):
            rows_all[stream, pl.ds(pl.multiple_of(p * 16, 16), 16), q * quarter:(q + 1) * quarter] = got[q * 16:(q + 1) * 16]

    def part(stream, row, size):
        return rows_all.at[stream, pl.ds(pl.multiple_of(row, 16), size)]

    sibs = [[], []]

    def to_sibling(stream, row, size):
        k = len(sibs[stream])
        ref = part(stream, row, size)
        sibs[stream].append(go(remote(ref, ref, sib_s.at[stream, k], sib_r.at[stream, k], e=sibling)))

    base = c * 128
    y_up, y_down, y_far = rem(y + 1, 4), rem(y + 3, 4), rem(y + 2, 4)

    def gather_1(stream):
        ref = part(stream, p * 16, 16)
        copy = go(remote(ref, ref, c1_s.at[stream], c1_r.at[stream], e=partner))
        to_sibling(stream, p * 16, 16)
        return copy

    def gather_2(stream, first):
        first.wait_recv()
        ref = part(stream, base + y * 32, 32)
        copies = [
            go(remote(ref, ref, c2_s.at[stream, 0], c2_r.at[stream, 0], e=up)),
            go(remote(ref, ref, c2_s.at[stream, 1], c2_r.at[stream, 1], e=down)),
        ]
        to_sibling(stream, base + y * 32 + (1 - xl) * 16, 16)
        return copies

    def gather_3(stream, second):
        second[0].wait_recv()
        low = part(stream, base + y_down * 32, 16)
        copies = [go(remote(low, low, c3_s.at[stream, 0], c3_r.at[stream, 0], e=up))]
        second[1].wait_recv()
        high = part(stream, base + y_up * 32 + 16, 16)
        copies.append(go(remote(high, high, c3_s.at[stream, 1], c3_r.at[stream, 1], e=down)))
        to_sibling(stream, base + y_down * 32, 32)
        to_sibling(stream, base + y_up * 32, 32)
        return copies

    def gather_4(stream, third):
        for copy in third:
            copy.wait_recv()
        to_sibling(stream, base + y_far * 32, 32)

    unpack(0)
    first_x = gather_1(0)
    second_x = gather_2(0, first_x)
    third_x = gather_3(0, second_x)
    unpack(1)
    first_g = gather_1(1)
    gather_4(0, third_x)
    second_g = gather_2(1, first_g)
    for copy in sibs[0]:
        copy.wait_recv()
    loads[2].wait()
    preact = jnp.zeros((256, win.shape[1]), F32)
    for k in range(4):
        cols = slice(k * quarter, (k + 1) * quarter)
        preact = preact + jnp.dot(rows_all[0, :, cols], win[cols, :], preferred_element_type=F32)
    third_g = gather_3(1, second_g)
    square = preact * preact
    th = jnp.tanh(K0 * preact * (1.0 + K1 * square))
    hid[...] = (0.5 * preact * (1.0 + th)).astype(BF16)
    slope = 0.5 * (1.0 + th) + 0.5 * preact * (1.0 - th * th) * (K0 * (1.0 + 3.0 * K1 * square))
    gather_4(1, third_g)
    for copy in sibs[1]:
        copy.wait_recv()
    loads[3].wait()
    post = jnp.zeros((256, wout.shape[0]), F32)
    for k in range(4):
        cols = slice(k * quarter, (k + 1) * quarter)
        post = post + lax.dot_general(rows_all[1, :, cols], wout[:, cols], NT, preferred_element_type=F32)
    pre_grad[...] = (post * slope).astype(BF16)

    half = width // 2
    e1 = []
    for h in range(2):
        theirs = pre_grad[pl.ds(pl.multiple_of((1 - c) * 128, 128), 128), :]
        for k in range(2):
            cols = slice(h * half + k * quarter, h * half + (k + 1) * quarter)
            e1s[h, :, k * quarter:(k + 1) * quarter] = lax.dot_general(
                theirs, win[cols, :], NT, preferred_element_type=F32).astype(BF16)
        e1.append(go(remote(e1s.at[h], e1r.at[h], e1_ss.at[h], e1_rs.at[h], e=sibling)))
    for h in range(2):
        ours = pre_grad[pl.ds(pl.multiple_of(c * 128, 128), 128), :]
        for k in range(2):
            cols = slice(h * half + k * quarter, h * half + (k + 1) * quarter)
            q_ref[h, :, k * quarter:(k + 1) * quarter] = lax.dot_general(
                ours, win[cols, :], NT, preferred_element_type=F32)

    def q_rows(h, row, size):
        return q_ref[h, pl.ds(pl.multiple_of(row, 16), size), :]

    e2, e3 = [], []
    for h in range(2):
        e1[h].wait_recv()
        q_ref[h] = q_ref[h] + e1r[h].astype(F32)
        for k, target in enumerate((up, down)):
            e2s[h, k] = q_rows(h, y_far * 32 + k * 16, 16).astype(BF16)
            e2.append(go(remote(e2s.at[h, k], e2r.at[h, k], e2_ss.at[h, k], e2_rs.at[h, k], e=target)))
        for k, (target, yt) in enumerate(((up, y_up), (down, y_down))):
            other = 1 - k
            e3s[h, k, other] = q_rows(h, yt * 32 + other * 16, 16).astype(BF16)
            e3.append(go(remote(e3s.at[h, k, other], e3r.at[h, k, other], e3_ss.at[h, k, other], e3_rs.at[h, k, other], e=target)))
    for h in range(2):
        for k, (target, yt) in enumerate(((up, y_up), (down, y_down))):
            e2[2 * h + k].wait_recv()
            e3s[h, k, k] = (q_rows(h, yt * 32 + k * 16, 16) + e2r[h, k].astype(F32)).astype(BF16)
            e3.append(go(remote(e3s.at[h, k, k], e3r.at[h, k, k], e3_ss.at[h, k, k], e3_rs.at[h, k, k], e=target)))

    turned = hid[...].astype(F32).T.astype(BF16)
    for k in range(4):
        cols = slice(k * quarter, (k + 1) * quarter)
        wog[:, cols] = jnp.dot(turned, rows_all[1, :, cols], preferred_element_type=F32).astype(BF16)
    store = pltpu.make_async_copy(wog, wog_hbm, ld_sem.at[4])
    store.start()

    e4 = []
    for h in range(2):
        for copy in (e3[2 * h], e3[2 * h + 1], e3[4 + 2 * h], e3[5 + 2 * h]):
            copy.wait_recv()
        total = q_rows(h, y * 32, 32)
        for k in range(2):
            total = total + jnp.concatenate([e3r[h, k, 0], e3r[h, k, 1]], axis=0).astype(F32)
        q_ref[h, pl.ds(pl.multiple_of(y * 32, 32), 32), :] = total
        e4s[h] = q_rows(h, y * 32 + (1 - xl) * 16, 16).astype(BF16)
        e4.append(go(remote(e4s.at[h], e4r.at[h], e4_ss.at[h], e4_rs.at[h], e=partner)))

    eighth = width // 8
    f_copies = []
    for h in range(2):
        e4[h].wait_recv()
        total = (q_rows(h, y * 32 + xl * 16, 16) + e4r[h].astype(F32)).astype(BF16)
        stacked = jnp.concatenate([total[:, q * eighth:(q + 1) * eighth] for q in range(4)], axis=0)
        fs[h] = jnp.dot(swap, stacked, preferred_element_type=F32).astype(BF16)
        row = []
        for j in (1, 3, 0, 2):
            copy = exchange(block(fs.at[h], j), block(fr.at[h], j), f_ss.at[h, j], f_rs.at[h, j], source[j], j == 2)
            row.append(copy)
            if j == 2:
                guarded.append(copy)
        f_copies.append(row)

    t_copies = []
    for h in range(2):
        for copy in f_copies[h]:
            copy.wait_recv()
        got = jnp.dot(swap, fr[h], preferred_element_type=F32).astype(BF16)
        for k in range(8):
            ts[h * 8 + k] = got[(k // 2) * 16:(k // 2 + 1) * 16, (k % 2) * 128:(k % 2 + 1) * 128]
        for k in range(8):
            target = h * 8 + rem(k + m, 8)
            src, dst = ts.at[target], tr.at[pl.ds(pl.multiple_of(p * 16, 16), 16)]
            copy = remote(src, dst, t_ss.at[target], t_rs.at[p], e=target)

            @pl.when(target != m)
            def _():
                copy.start()

            @pl.when(target == m)
            def _():
                pltpu.make_async_copy(src, dst, t_rs.at[p]).start()

            t_copies.append((target, copy))

    for q in range(PLANE):
        remote(ts.at[0], tr.at[pl.ds(q * 16, 16)], t_ss.at[0], t_rs.at[q]).wait_recv()
    out_ref[...] = lax.dot_general(dall[...], tr[...], TN, preferred_element_type=F32).astype(BF16)

    for copy in waits:
        copy.wait_send()

    @pl.when(jnp.logical_not(to_self))
    def _():
        for copy in guarded:
            copy.wait_send()

    for target, copy in t_copies:
        @pl.when(target != m)
        def _():
            copy.wait_send()
    store.wait()


def shards(tokens, cotangent, gate_values, expert_ids, weight_in, weight_out):
    count, width = tokens.shape
    hidden = weight_in.shape[2]
    dma = pltpu.SemaphoreType.DMA
    half = width // 2
    vmem = pl.BlockSpec(memory_space=pltpu.VMEM)
    hbm = pl.BlockSpec(memory_space=pl.ANY)
    rows = PLANE * ROWS
    out, grad = pl.pallas_call(
        kernel,
        out_shape=(
            jax.ShapeDtypeStruct((count, width // PLANE), BF16),
            jax.ShapeDtypeStruct((hidden, width), BF16),
        ),
        in_specs=[hbm, hbm, vmem, vmem, hbm, hbm],
        out_specs=(vmem, hbm),
        scratch_shapes=[
            pltpu.VMEM((count, width), BF16),
            pltpu.VMEM((count, width), BF16),
            pltpu.VMEM((width, hidden), BF16),
            pltpu.VMEM((hidden, width), BF16),
            pltpu.VMEM((hidden, width), BF16),
            pltpu.VMEM((2, 64, width // 4), BF16),
            pltpu.VMEM((2, 64, width // 4), BF16),
            pltpu.VMEM((2, rows, width), BF16),
            pltpu.VMEM((rows, hidden), BF16),
            pltpu.VMEM((rows, hidden), BF16),
            pltpu.VMEM((2, rows // 2, half), BF16),
            pltpu.VMEM((2, rows // 2, half), BF16),
            pltpu.VMEM((2, rows // 2, half), F32),
            pltpu.VMEM((2, 2, 16, half), BF16),
            pltpu.VMEM((2, 2, 16, half), BF16),
            pltpu.VMEM((2, 2, 2, 16, half), BF16),
            pltpu.VMEM((2, 2, 2, 16, half), BF16),
            pltpu.VMEM((2, 16, half), BF16),
            pltpu.VMEM((2, 16, half), BF16),
            pltpu.VMEM((2, 64, half // 4), BF16),
            pltpu.VMEM((2, 64, half // 4), BF16),
            pltpu.VMEM((PLANE, 16, width // PLANE), BF16),
            pltpu.VMEM((rows, width // PLANE), BF16),
            pltpu.VMEM((rows, count), BF16),
            dma((5,)),
            dma((2, 4)), dma((2, 4)),
            dma((2,)), dma((2,)),
            dma((2, 2)), dma((2, 2)),
            dma((2, 2)), dma((2, 2)),
            dma((2, 5)), dma((2, 5)),
            dma((2,)), dma((2,)),
            dma((2, 2)), dma((2, 2)),
            dma((2, 2, 2)), dma((2, 2, 2)),
            dma((2,)), dma((2,)),
            dma((2, 4)), dma((2, 4)),
            dma((PLANE,)), dma((PLANE,)),
        ],
        compiler_params=pltpu.CompilerParams(
            collective_id=0, has_side_effects=True, vmem_limit_bytes=40 * 1024 * 1024
        ),
    )(tokens, cotangent, expert_ids.T, gate_values.T, weight_in[0], weight_out[0])
    return out, grad[None]


def solution(mesh):
    placed = (
        P("dp", None),
        P("dp", None),
        P("dp", None),
        P("dp", None),
        P("dp", None, "expert"),
        P("dp", "expert", None),
    )
    return jax.shard_map(
        shards,
        mesh=mesh,
        in_specs=placed,
        out_specs=(P("dp", "expert"), P("dp", "expert", None)),
        check_vma=False,
    )
```

```python
import functools

import jax
import jax.numpy as jnp
from jax import lax
from jax.experimental import pallas as pl
from jax.experimental.pallas import tpu as pltpu
from jax.sharding import PartitionSpec as P

CAP = 4
PLANE = 16
NZ = 32
F32 = jnp.float32
BF16 = jnp.bfloat16
NT = (((1,), (1,)), ((), ()))
TN = (((0,), (0,)), ((), ()))
K0 = 0.7978845608028654
K1 = 0.044715


def rem(a, b):
    return lax.rem(a, b)


def iota(shape, dim):
    return lax.broadcasted_iota(jnp.int32, shape, dim)


def offsets(s):
    return (s + 1, 32 - s, 8 - s, 25 + s, 16 - s, 17 + s, 9 + s, 24 - s)


def kernel(
    tok_hbm, cot_hbm, ids_ref, gate_ref, win_hbm, wout_hbm, out_ref, wog_hbm,
    tok, cot, win, wout, wog, tx, packed, x_ref, g_ref, g_sib, hid, hid_sib,
    es, er, q_ref, fs, fr, ts, tr, dall,
    ld_sem, b_s, b_r, w_s, w_r, ag_s, ag_r, g_ss, g_rs, h_ss, h_rs, e_ss, e_rs, f_ss, f_rs, t_ss, t_rs,
):
    half = tok.shape[1]
    piece = half // 4
    m = lax.axis_index("expert")
    d = lax.axis_index("dp")
    y, xl, c = m // 4, rem(m // 2, 2), rem(m, 2)
    xh, z = d // NZ, rem(d, NZ)
    s, fh = rem(y, 2) * 2 + xl, y // 2
    mine = rem(m, 8)
    off = offsets(s)
    xo = rem(xh + c, 2)
    dest = [xo * NZ + rem(z + o, NZ) for o in off]
    source = [xo * NZ + rem(z + NZ - o, NZ) for o in off]
    to_self = (s == 0) & (c == 0)
    sibling = m + 1 - 2 * c
    steps = [(dy, dx) for dy in (2, 1, 3, 0) for dx in (1, 0) if (dy, dx) != (0, 0)]

    def chip(dy, dx):
        ty, tx_ = rem(y + dy, 4), rem(xl + dx, 2)
        return rem(ty, 2) * 2 + tx_, ty // 2, ty * 4 + tx_ * 2 + c

    columns = pl.ds(pl.multiple_of(fh * half, 128), half)
    loads = [
        pltpu.make_async_copy(src, dst, ld_sem.at[i])
        for i, (src, dst) in enumerate(
            ((tok_hbm.at[:, columns], tok), (cot_hbm.at[:, columns], cot), (win_hbm, win.at[0]), (wout_hbm, wout.at[0])))
    ]
    for copy in loads:
        copy.start()
    barrier = pltpu.get_barrier_semaphore()

    def greet(e, dp):
        pl.semaphore_signal(barrier, inc=1, device_id={"expert": e, "dp": dp}, device_id_type=pl.DeviceIdType.MESH)

    order = (4, 5, 6, 7, 2, 3, 0)
    for i in order:
        greet(m, dest[i])
        greet(m, source[i])

    @pl.when(jnp.logical_not(to_self))
    def _():
        greet(m, dest[1])
        greet(m, source[1])

    for dy, dx in steps:
        greet(chip(dy, dx)[2], d)
    for k in (1, 3, 5, 7):
        greet(fh * 8 + rem(mine + k, 8), d)

    id0, id1 = ids_ref[0:1, :], ids_ref[1:2, :]
    g0, g1 = gate_ref[0:1, :], gate_ref[1:2, :]
    count = id0.shape[1]
    earlier = (iota((count, count), 0) < iota((count, count), 1)).astype(BF16)

    def slots(expert, slot):
        one0, one1 = id0 == expert, id1 == expert
        one = one0 | one1
        before = jnp.dot(one.astype(F32).astype(BF16), earlier, preferred_element_type=F32)
        taken = one & (before.astype(jnp.int32) == slot)
        return taken, one0

    r = iota((128, 1), 0)
    ri, rq, rs = r // 16, rem(r // 4, 4), rem(r, 4)
    expert = jnp.zeros_like(r)
    for i in range(8):
        expert = jnp.where(ri == i, dest[i], expert)
    taken, one0 = slots(expert, rs)
    gate = jnp.sum(jnp.where(taken, jnp.where(one0, g0, g1), 0.0), axis=1, keepdims=True)
    picks = [(taken & (rq == q)).astype(F32).astype(BF16) for q in range(4)]

    def fill(stream, ref, scale):
        total = None
        for q in range(4):
            part = jnp.dot(picks[q], ref[:, q * piece:(q + 1) * piece], preferred_element_type=F32)
            total = part if total is None else total + part
        if scale is not None:
            total = total * scale
        tx[stream] = total.astype(BF16)

    loads[0].wait()
    fill(0, tok, None)
    loads[1].wait()
    fill(1, cot, gate)
    pl.semaphore_wait(barrier, 16 + 7 + 4 - 2 * to_self.astype(jnp.int32))

    waits, guarded = [], []

    def remote(src, dst, send, recv, e=None, dp=None):
        return pltpu.make_async_remote_copy(
            src_ref=src, dst_ref=dst, send_sem=send, recv_sem=recv,
            device_id={"expert": m if e is None else e, "dp": d if dp is None else dp},
            device_id_type=pl.DeviceIdType.MESH,
        )

    def go(copy):
        copy.start()
        waits.append(copy)
        return copy

    def exchange(src, dst, send, recv, dp, is_self):
        copy = remote(src, dst, send, recv, dp=dp)
        if not is_self:
            return go(copy)

        @pl.when(jnp.logical_not(to_self))
        def _():
            copy.start()

        @pl.when(to_self)
        def _():
            pltpu.make_async_copy(src, dst, recv).start()

        guarded.append(copy)
        return copy

    def block(ref, row, size=16):
        return ref.at[pl.ds(row if isinstance(row, int) else pl.multiple_of(row, 16), size)]

    b_copies = {}
    for way, order in ((1, (4, 5, 6, 7)), (0, (2, 3, 0, 1))):
        for stream in range(2):
            for i in order:
                b_copies[stream, i] = exchange(
                    block(tx.at[stream], i * 16), block(packed.at[stream, way, fh], s * 64 + (i % 4) * 16),
                    b_s.at[stream, i], b_r.at[stream, i], dest[i], i == 1)

    weights = []
    for i, ref in enumerate((win, wout)):
        loads[2 + i].wait()
        weights.append(go(remote(ref.at[0], ref.at[1], w_s.at[i], w_r.at[i], e=sibling)))

    def matrix(n, same):
        return same(iota((n, n), 0), iota((n, n), 1)).astype(F32).astype(BF16)

    spread = matrix(256, lambda t, u: (t // 64 == rem(u // 4, 4)) & (rem(t // 4, 16) == u // 16) & (rem(t, 4) == rem(u, 4)))
    swap = matrix(64, lambda t, u: (t // 16 == rem(u // 4, 4)) & (rem(t // 4, 4) == u // 16) & (rem(t, 4) == rem(u, 4)))

    ar = iota((256, 1), 0)
    at, ai, asl = ar // 32, rem(ar // 4, 8), rem(ar, 4)
    aoff = jnp.zeros_like(ar)
    for i, o in enumerate(offsets(at // 2)):
        aoff = jnp.where(ai == i, o, aoff)
    all_taken, _ = slots(rem(xh + rem(at, 2), 2) * NZ + rem(z + aoff, NZ), asl)
    dall[...] = all_taken.astype(F32).astype(BF16)

    for way in range(2):
        for stream in range(2):
            for i in range(4 * way, 4 * way + 4):
                b_copies[stream, i].wait_recv()
            ref = block(packed.at[stream, way, fh], s * 64, 64)
            for k, step in enumerate(steps):
                go(remote(ref, ref, ag_s.at[stream, way, k], ag_r.at[stream, way, fh, s], e=chip(*step)[2]))

    def unpack(stream, way, target):
        for step in reversed(steps):
            ts_, tf, _ = chip(*step)
            ref = block(packed.at[stream, way, tf], ts_ * 64, 64)
            remote(ref, ref, ag_s.at[stream, way, 0], ag_r.at[stream, way, tf, ts_], e=sibling).wait_recv()
        for f in range(2):
            got = jnp.dot(spread, packed[stream, way, f], preferred_element_type=F32).astype(BF16)
            for q in range(4):
                cols = slice(f * half + q * piece, f * half + (q + 1) * piece)
                target[way * 64:(way + 1) * 64, cols] = got[q * 64:(q + 1) * 64]

    chunk = half // 2
    e_copies = []
    for way in range(2):
        rows = slice(way * 64, (way + 1) * 64)
        unpack(0, way, x_ref)
        if way == 0:
            weights[0].wait_recv()
        slopes = []
        for i in range(2):
            preact = None
            for k in range(4):
                cols = slice(k * chunk, (k + 1) * chunk)
                part = jnp.dot(x_ref[rows, cols], win[i, cols, :], preferred_element_type=F32)
                preact = part if preact is None else preact + part
            square = preact * preact
            th = jnp.tanh(K0 * preact * (1.0 + K1 * square))
            hid[i, rows, :] = (0.5 * preact * (1.0 + th)).astype(BF16)
            slopes.append(0.5 * (1.0 + th) + 0.5 * preact * (1.0 - th * th) * (K0 * (1.0 + 3.0 * K1 * square)))
        unpack(1, way, g_ref)
        if way == 0:
            weights[1].wait_recv()
        grads = []
        for i in range(2):
            post = None
            for k in range(4):
                cols = slice(k * chunk, (k + 1) * chunk)
                part = lax.dot_general(g_ref[rows, cols], wout[i, :, cols], NT, preferred_element_type=F32)
                post = part if post is None else post + part
            grads.append((post * slopes[i]).astype(BF16))
        for k in range(4):
            cols = slice(k * chunk, (k + 1) * chunk)
            part = lax.dot_general(grads[0], win[0, cols, :], NT, preferred_element_type=F32)
            part = part + lax.dot_general(grads[1], win[1, cols, :], NT, preferred_element_type=F32)
            here = slice((k % 2) * chunk, (k % 2 + 1) * chunk)
            q_ref[way, k // 2, :, here] = part
            es[way, k // 2, :, here] = part.astype(BF16)
        row = []
        for k, step in enumerate(steps):
            ts_, tf, e = chip(*step)
            row.append(go(remote(
                block(es.at[way, tf], ts_ * 16), er.at[way, k], e_ss.at[way, k], e_rs.at[way, k], e=e)))
        e_copies.append(row)

    g_copy = go(remote(g_ref, g_sib, g_ss, g_rs, e=sibling))
    hid_copy = go(remote(hid.at[1], hid_sib, h_ss, h_rs, e=sibling))

    f_copies = []
    for way in range(2):
        total = q_ref[way, fh, pl.ds(pl.multiple_of(s * 16, 16), 16), :]
        for k in reversed(range(len(steps))):
            e_copies[way][k].wait_recv()
            total = total + er[way, k].astype(F32)
        total = total.astype(BF16)
        stacked = jnp.concatenate([total[:, q * piece:(q + 1) * piece] for q in range(4)], axis=0)
        fs[way] = jnp.dot(swap, stacked, preferred_element_type=F32).astype(BF16)
        f_copies.append([
            exchange(block(fs.at[way], j * 16), block(fr.at[way], j * 16), f_ss.at[way, j], f_rs.at[way, j],
                     source[4 * way + j], way == 0 and j == 1)
            for j in range(4)
        ])

    hid_copy.wait_recv()
    turned = jnp.concatenate([hid[0].astype(F32).T, hid_sib[...].astype(F32).T], axis=1).astype(BF16)
    g_copy.wait_recv()
    for k in range(4):
        cols = slice(k * chunk, (k + 1) * chunk)
        both = jnp.concatenate([g_ref[:, cols], g_sib[:, cols]], axis=0)
        wog[:, cols] = jnp.dot(turned, both, preferred_element_type=F32).astype(BF16)
    store = pltpu.make_async_copy(wog, wog_hbm, ld_sem.at[4])
    store.start()

    t_copies = []
    for way in range(2):
        for copy in f_copies[way]:
            copy.wait_recv()
        got = jnp.dot(swap, fr[way], preferred_element_type=F32).astype(BF16)
        for k in range(8):
            ts[way, k] = got[(k // 2) * 16:(k // 2 + 1) * 16, (k % 2) * 128:(k % 2 + 1) * 128]
        for k in range(1, 8):
            there = rem(mine + k, 8)
            t_copies.append(go(remote(
                ts.at[way, there], block(tr, mine * 32 + way * 16), t_ss.at[way, k], t_rs.at[way, k], e=fh * 8 + there)))
        tr[pl.ds(pl.multiple_of(mine * 32 + way * 16, 16), 16), :] = ts[way, mine]

    for copy in t_copies:
        copy.wait_recv()
    out_ref[...] = lax.dot_general(dall[...], tr[...], TN, preferred_element_type=F32).astype(BF16)

    for copy in waits:
        copy.wait_send()

    @pl.when(jnp.logical_not(to_self))
    def _():
        for copy in guarded:
            copy.wait_send()

    store.wait()


def shards(tokens, cotangent, gate_values, expert_ids, weight_in, weight_out):
    count, width = tokens.shape
    hidden = weight_in.shape[2]
    dma = pltpu.SemaphoreType.DMA
    half = width // 2
    vmem = pl.BlockSpec(memory_space=pltpu.VMEM)
    hbm = pl.BlockSpec(memory_space=pltpu.HBM)
    out, grad = pl.pallas_call(
        kernel,
        out_shape=(
            jax.ShapeDtypeStruct((count, width // PLANE), BF16),
            jax.ShapeDtypeStruct((hidden, width), BF16),
        ),
        in_specs=[hbm, hbm, vmem, vmem, hbm, hbm],
        out_specs=(vmem, hbm),
        scratch_shapes=[
            pltpu.VMEM((count, half), BF16),
            pltpu.VMEM((count, half), BF16),
            pltpu.VMEM((2, width, hidden), BF16),
            pltpu.VMEM((2, hidden, width), BF16),
            pltpu.VMEM((hidden, width), BF16),
            pltpu.VMEM((2, 128, half // 4), BF16),
            pltpu.VMEM((2, 2, 2, 256, half // 4), BF16),
            pltpu.VMEM((128, width), BF16),
            pltpu.VMEM((128, width), BF16),
            pltpu.VMEM((128, width), BF16),
            pltpu.VMEM((2, 128, hidden), BF16),
            pltpu.VMEM((128, hidden), BF16),
            pltpu.VMEM((2, 2, 64, half), BF16),
            pltpu.VMEM((2, 7, 16, half), BF16),
            pltpu.VMEM((2, 2, 64, half), F32),
            pltpu.VMEM((2, 64, half // 4), BF16),
            pltpu.VMEM((2, 64, half // 4), BF16),
            pltpu.VMEM((2, 8, 16, width // PLANE), BF16),
            pltpu.VMEM((256, width // PLANE), BF16),
            pltpu.VMEM((256, count), BF16),
            dma((5,)),
            dma((2, 8)), dma((2, 8)),
            dma((2,)), dma((2,)),
            dma((2, 2, 7)), dma((2, 2, 2, 4)),
            dma, dma,
            dma, dma,
            dma((2, 7)), dma((2, 7)),
            dma((2, 4)), dma((2, 4)),
            dma((2, 8)), dma((2, 8)),
        ],
        compiler_params=pltpu.CompilerParams(
            collective_id=0, has_side_effects=True, vmem_limit_bytes=63 * 1024 * 1024
        ),
    )(tokens, cotangent, expert_ids.T, gate_values.T, weight_in[0], weight_out[0])
    return out, grad[None]


def solution(mesh):
    placed = (
        P("dp", None),
        P("dp", None),
        P("dp", None),
        P("dp", None),
        P("dp", None, "expert"),
        P("dp", "expert", None),
    )
    return jax.shard_map(
        shards,
        mesh=mesh,
        in_specs=placed,
        out_specs=(P("dp", "expert"), P("dp", "expert", None)),
        check_vma=False,
    )
```

```python
import functools

import jax
import jax.numpy as jnp
from jax import lax
from jax.experimental import pallas as pl
from jax.experimental.pallas import tpu as pltpu
from jax.sharding import PartitionSpec as P

CAP = 4
PLANE = 16
NZ = 32
F32 = jnp.float32
BF16 = jnp.bfloat16
NT = (((1,), (1,)), ((), ()))
TN = (((0,), (0,)), ((), ()))
K0 = 0.7978845608028654
K1 = 0.044715


def rem(a, b):
    return lax.rem(a, b)


def iota(shape, dim):
    return lax.broadcasted_iota(jnp.int32, shape, dim)


def offsets(s):
    return (s + 1, 32 - s, 8 - s, 25 + s, 16 - s, 17 + s, 9 + s, 24 - s)


def kernel(
    tok_hbm, cot_hbm, ids_ref, gate_ref, win_hbm, wout_hbm, out_ref, wog,
    tok, cot, win, wout, tx, packed, x_ref, g_ref, g_sib, hid, hid_sib,
    es, er, q_ref, fs, fr, ts, tr, dall,
    ld_sem, b_s, b_r, w_s, w_r, ag_s, ag_r, g_ss, g_rs, h_ss, h_rs, e_ss, e_rs, f_ss, f_rs, t_ss, t_rs,
):
    half = tok.shape[1]
    piece = half // 4
    m = lax.axis_index("expert")
    d = lax.axis_index("dp")
    y, xl, c = m // 4, rem(m // 2, 2), rem(m, 2)
    xh, z = d // NZ, rem(d, NZ)
    s, fh = rem(y, 2) * 2 + xl, y // 2
    mine = rem(m, 8)
    off = offsets(s)
    xo = rem(xh + c, 2)
    dest = [xo * NZ + rem(z + o, NZ) for o in off]
    source = [xo * NZ + rem(z + NZ - o, NZ) for o in off]
    to_self = (s == 0) & (c == 0)
    sibling = m + 1 - 2 * c
    steps = [(dy, dx) for dy in (2, 1, 3, 0) for dx in (1, 0) if (dy, dx) != (0, 0)]

    def chip(dy, dx):
        ty, tx_ = rem(y + dy, 4), rem(xl + dx, 2)
        return rem(ty, 2) * 2 + tx_, ty // 2, ty * 4 + tx_ * 2 + c

    columns = pl.ds(pl.multiple_of(fh * half, 128), half)
    loads = [
        pltpu.make_async_copy(src, dst, ld_sem.at[i])
        for i, (src, dst) in enumerate(
            ((tok_hbm.at[:, columns], tok), (cot_hbm.at[:, columns], cot), (win_hbm, win.at[0]), (wout_hbm, wout.at[0])))
    ]
    for copy in loads:
        copy.start()
    barrier = pltpu.get_barrier_semaphore()

    def greet(e, dp):
        pl.semaphore_signal(barrier, inc=1, device_id={"expert": e, "dp": dp}, device_id_type=pl.DeviceIdType.MESH)

    order = (4, 5, 6, 7, 2, 3, 0)
    for i in order:
        greet(m, dest[i])
        greet(m, source[i])

    @pl.when(jnp.logical_not(to_self))
    def _():
        greet(m, dest[1])
        greet(m, source[1])

    for dy, dx in steps:
        greet(chip(dy, dx)[2], d)
    for k in (1, 3, 5, 7):
        greet(fh * 8 + rem(mine + k, 8), d)

    id0, id1 = ids_ref[0:1, :], ids_ref[1:2, :]
    g0, g1 = gate_ref[0:1, :], gate_ref[1:2, :]
    count = id0.shape[1]
    earlier = (iota((count, count), 0) < iota((count, count), 1)).astype(BF16)

    def slots(expert, slot):
        one0, one1 = id0 == expert, id1 == expert
        one = one0 | one1
        before = jnp.dot(one.astype(F32).astype(BF16), earlier, preferred_element_type=F32)
        taken = one & (before.astype(jnp.int32) == slot)
        return taken, one0

    r = iota((128, 1), 0)
    ri, rq, rs = r // 16, rem(r // 4, 4), rem(r, 4)
    expert = jnp.zeros_like(r)
    for i in range(8):
        expert = jnp.where(ri == i, dest[i], expert)
    taken, one0 = slots(expert, rs)
    gate = jnp.sum(jnp.where(taken, jnp.where(one0, g0, g1), 0.0), axis=1, keepdims=True)
    picks = [(taken & (rq == q)).astype(F32).astype(BF16) for q in range(4)]

    def fill(stream, ref, scale):
        total = None
        for q in range(4):
            part = jnp.dot(picks[q], ref[:, q * piece:(q + 1) * piece], preferred_element_type=F32)
            total = part if total is None else total + part
        if scale is not None:
            total = total * scale
        tx[stream] = total.astype(BF16)

    loads[0].wait()
    fill(0, tok, None)
    loads[1].wait()
    fill(1, cot, gate)
    pl.semaphore_wait(barrier, 16 + 7 + 4 - 2 * to_self.astype(jnp.int32))

    waits, guarded = [], []

    def remote(src, dst, send, recv, e=None, dp=None):
        return pltpu.make_async_remote_copy(
            src_ref=src, dst_ref=dst, send_sem=send, recv_sem=recv,
            device_id={"expert": m if e is None else e, "dp": d if dp is None else dp},
            device_id_type=pl.DeviceIdType.MESH,
        )

    def go(copy):
        copy.start()
        waits.append(copy)
        return copy

    def exchange(src, dst, send, recv, dp, is_self):
        copy = remote(src, dst, send, recv, dp=dp)
        if not is_self:
            return go(copy)

        @pl.when(jnp.logical_not(to_self))
        def _():
            copy.start()

        @pl.when(to_self)
        def _():
            pltpu.make_async_copy(src, dst, recv).start()

        guarded.append(copy)
        return copy

    def block(ref, row, size=16):
        return ref.at[pl.ds(row if isinstance(row, int) else pl.multiple_of(row, 16), size)]

    b_copies = {}

    def send_b(way, order):
        for stream in range(2):
            for i in order:
                b_copies[stream, i] = exchange(
                    block(tx.at[stream], i * 16), block(packed.at[stream, way, fh], s * 64 + (i % 4) * 16),
                    b_s.at[stream, i], b_r.at[stream, i], dest[i], i == 1)

    send_b(1, (4, 5, 6, 7))

    weights = []
    for i, ref in enumerate((win, wout)):
        loads[2 + i].wait()
        weights.append(go(remote(ref.at[0], ref.at[1], w_s.at[i], w_r.at[i], e=sibling)))

    def matrix(n, same):
        return same(iota((n, n), 0), iota((n, n), 1)).astype(F32).astype(BF16)

    spread = matrix(256, lambda t, u: (t // 64 == rem(u // 4, 4)) & (rem(t // 4, 16) == u // 16) & (rem(t, 4) == rem(u, 4)))
    swap = matrix(64, lambda t, u: (t // 16 == rem(u // 4, 4)) & (rem(t // 4, 4) == u // 16) & (rem(t, 4) == rem(u, 4)))

    ar = iota((256, 1), 0)
    at, ai, asl = ar // 32, rem(ar // 4, 8), rem(ar, 4)
    aoff = jnp.zeros_like(ar)
    for i, o in enumerate(offsets(at // 2)):
        aoff = jnp.where(ai == i, o, aoff)
    all_taken, _ = slots(rem(xh + rem(at, 2), 2) * NZ + rem(z + aoff, NZ), asl)
    dall[...] = all_taken.astype(F32).astype(BF16)

    send_b(0, (2, 3, 0, 1))

    for way in range(2):
        for stream in range(2):
            for i in range(4 * way, 4 * way + 4):
                b_copies[stream, i].wait_recv()
            ref = block(packed.at[stream, way, fh], s * 64, 64)
            for k, step in enumerate(steps):
                go(remote(ref, ref, ag_s.at[stream, way, k], ag_r.at[stream, way, fh, s], e=chip(*step)[2]))

    def unpack(stream, way, target):
        for step in reversed(steps):
            ts_, tf, _ = chip(*step)
            ref = block(packed.at[stream, way, tf], ts_ * 64, 64)
            remote(ref, ref, ag_s.at[stream, way, 0], ag_r.at[stream, way, tf, ts_], e=sibling).wait_recv()
        for f in range(2):
            got = jnp.dot(spread, packed[stream, way, f], preferred_element_type=F32).astype(BF16)
            for q in range(4):
                cols = slice(f * half + q * piece, f * half + (q + 1) * piece)
                target[way * 64:(way + 1) * 64, cols] = got[q * 64:(q + 1) * 64]

    chunk = half // 2
    e_copies = []
    for way in range(2):
        rows = slice(way * 64, (way + 1) * 64)
        unpack(0, way, x_ref)
        if way == 0:
            weights[0].wait_recv()
        slopes = []
        for i in range(2):
            preact = None
            for k in range(4):
                cols = slice(k * chunk, (k + 1) * chunk)
                part = jnp.dot(x_ref[rows, cols], win[i, cols, :], preferred_element_type=F32)
                preact = part if preact is None else preact + part
            square = preact * preact
            th = jnp.tanh(K0 * preact * (1.0 + K1 * square))
            hid[i, rows, :] = (0.5 * preact * (1.0 + th)).astype(BF16)
            slopes.append(0.5 * (1.0 + th) + 0.5 * preact * (1.0 - th * th) * (K0 * (1.0 + 3.0 * K1 * square)))
        unpack(1, way, g_ref)
        if way == 0:
            weights[1].wait_recv()
        grads = []
        for i in range(2):
            post = None
            for k in range(4):
                cols = slice(k * chunk, (k + 1) * chunk)
                part = lax.dot_general(g_ref[rows, cols], wout[i, :, cols], NT, preferred_element_type=F32)
                post = part if post is None else post + part
            grads.append((post * slopes[i]).astype(BF16))
        for k in range(4):
            cols = slice(k * chunk, (k + 1) * chunk)
            part = lax.dot_general(grads[0], win[0, cols, :], NT, preferred_element_type=F32)
            part = part + lax.dot_general(grads[1], win[1, cols, :], NT, preferred_element_type=F32)
            here = slice((k % 2) * chunk, (k % 2 + 1) * chunk)
            q_ref[way, k // 2, :, here] = part
            es[way, k // 2, :, here] = part.astype(BF16)
        row = []
        for k, step in enumerate(steps):
            ts_, tf, e = chip(*step)
            row.append(go(remote(
                block(es.at[way, tf], ts_ * 16), er.at[way, k], e_ss.at[way, k], e_rs.at[way, k], e=e)))
        e_copies.append(row)

    g_copy = go(remote(g_ref, g_sib, g_ss, g_rs, e=sibling))
    hid_copy = go(remote(hid.at[1], hid_sib, h_ss, h_rs, e=sibling))

    f_copies = []
    for way in range(2):
        total = q_ref[way, fh, pl.ds(pl.multiple_of(s * 16, 16), 16), :]
        for k in reversed(range(len(steps))):
            e_copies[way][k].wait_recv()
            total = total + er[way, k].astype(F32)
        total = total.astype(BF16)
        stacked = jnp.concatenate([total[:, q * piece:(q + 1) * piece] for q in range(4)], axis=0)
        fs[way] = jnp.dot(swap, stacked, preferred_element_type=F32).astype(BF16)
        f_copies.append([
            exchange(block(fs.at[way], j * 16), block(fr.at[way], j * 16), f_ss.at[way, j], f_rs.at[way, j],
                     source[4 * way + j], way == 0 and j == 1)
            for j in range(4)
        ])

    hid_copy.wait_recv()
    turned = jnp.concatenate([hid[0].astype(F32).T, hid_sib[...].astype(F32).T], axis=1).astype(BF16)
    g_copy.wait_recv()
    for k in range(4):
        cols = slice(k * chunk, (k + 1) * chunk)
        both = jnp.concatenate([g_ref[:, cols], g_sib[:, cols]], axis=0)
        wog[:, cols] = jnp.dot(turned, both, preferred_element_type=F32).astype(BF16)

    t_copies = []
    for way in range(2):
        for copy in f_copies[way]:
            copy.wait_recv()
        got = jnp.dot(swap, fr[way], preferred_element_type=F32).astype(BF16)
        for k in range(8):
            ts[way, k] = got[(k // 2) * 16:(k // 2 + 1) * 16, (k % 2) * 128:(k % 2 + 1) * 128]
        for k in range(1, 8):
            there = rem(mine + k, 8)
            t_copies.append(go(remote(
                ts.at[way, there], block(tr, mine * 32 + way * 16), t_ss.at[way, k], t_rs.at[way, k], e=fh * 8 + there)))
        tr[pl.ds(pl.multiple_of(mine * 32 + way * 16, 16), 16), :] = ts[way, mine]

    for copy in t_copies:
        copy.wait_recv()
    out_ref[...] = lax.dot_general(dall[...], tr[...], TN, preferred_element_type=F32).astype(BF16)

    for copy in waits:
        copy.wait_send()

    @pl.when(jnp.logical_not(to_self))
    def _():
        for copy in guarded:
            copy.wait_send()


def shards(tokens, cotangent, gate_values, expert_ids, weight_in, weight_out):
    count, width = tokens.shape
    hidden = weight_in.shape[2]
    dma = pltpu.SemaphoreType.DMA
    half = width // 2
    vmem = pl.BlockSpec(memory_space=pltpu.VMEM)
    hbm = pl.BlockSpec(memory_space=pltpu.HBM)
    out, grad = pl.pallas_call(
        kernel,
        out_shape=(
            pltpu.VMEM((count, width // PLANE), BF16),
            pltpu.VMEM((hidden, width), BF16),
        ),
        in_specs=[hbm, hbm, vmem, vmem, hbm, hbm],
        out_specs=(vmem, vmem),
        scratch_shapes=[
            pltpu.VMEM((count, half), BF16),
            pltpu.VMEM((count, half), BF16),
            pltpu.VMEM((2, width, hidden), BF16),
            pltpu.VMEM((2, hidden, width), BF16),
            pltpu.VMEM((2, 128, half // 4), BF16),
            pltpu.VMEM((2, 2, 2, 256, half // 4), BF16),
            pltpu.VMEM((128, width), BF16),
            pltpu.VMEM((128, width), BF16),
            pltpu.VMEM((128, width), BF16),
            pltpu.VMEM((2, 128, hidden), BF16),
            pltpu.VMEM((128, hidden), BF16),
            pltpu.VMEM((2, 2, 64, half), BF16),
            pltpu.VMEM((2, 7, 16, half), BF16),
            pltpu.VMEM((2, 2, 64, half), F32),
            pltpu.VMEM((2, 64, half // 4), BF16),
            pltpu.VMEM((2, 64, half // 4), BF16),
            pltpu.VMEM((2, 8, 16, width // PLANE), BF16),
            pltpu.VMEM((256, width // PLANE), BF16),
            pltpu.VMEM((256, count), BF16),
            dma((4,)),
            dma((2, 8)), dma((2, 8)),
            dma((2,)), dma((2,)),
            dma((2, 2, 7)), dma((2, 2, 2, 4)),
            dma, dma,
            dma, dma,
            dma((2, 7)), dma((2, 7)),
            dma((2, 4)), dma((2, 4)),
            dma((2, 8)), dma((2, 8)),
        ],
        compiler_params=pltpu.CompilerParams(
            collective_id=0, has_side_effects=True, vmem_limit_bytes=58 * 1024 * 1024
        ),
    )(tokens, cotangent, expert_ids.T, gate_values.T, weight_in[0], weight_out[0])
    return out, grad[None]


def solution(mesh):
    placed = (
        P("dp", None),
        P("dp", None),
        P("dp", None),
        P("dp", None),
        P("dp", None, "expert"),
        P("dp", "expert", None),
    )
    return jax.shard_map(
        shards,
        mesh=mesh,
        in_specs=placed,
        out_specs=(P("dp", "expert"), P("dp", "expert", None)),
        check_vma=False,
    )
```

```python
import functools

import jax
import jax.numpy as jnp
from jax import lax
from jax.experimental import pallas as pl
from jax.experimental.pallas import tpu as pltpu
from jax.sharding import PartitionSpec as P

CAP = 4
PLANE = 16
NZ = 32
F32 = jnp.float32
BF16 = jnp.bfloat16
NT = (((1,), (1,)), ((), ()))
TN = (((0,), (0,)), ((), ()))
K0 = 0.7978845608028654
K1 = 0.044715


def rem(a, b):
    return lax.rem(a, b)


def iota(shape, dim):
    return lax.broadcasted_iota(jnp.int32, shape, dim)


def offsets(s):
    return (s + 1, 32 - s, 8 - s, 25 + s, 16 - s, 17 + s, 9 + s, 24 - s)


def kernel(
    tok_hbm, cot_hbm, ids_ref, gate_ref, win_hbm, wout_hbm, out_ref, wog,
    tok, cot, win, wout, tx, packed, x_ref, g_ref, g_sib, hid, hid_sib,
    es, er, q_ref, fs, fr, ts, tr, dall,
    ld_sem, b_s, b_r, w_s, w_r, ag_s, ag_r, g_ss, g_rs, h_ss, h_rs, e_ss, e_rs, f_ss, f_rs, t_ss, t_rs,
):
    half = tok.shape[1]
    piece = half // 4
    m = lax.axis_index("expert")
    d = lax.axis_index("dp")
    y, xl, c = m // 4, rem(m // 2, 2), rem(m, 2)
    xh, z = d // NZ, rem(d, NZ)
    s, fh = rem(y, 2) * 2 + xl, y // 2
    mine = rem(m, 8)
    off = offsets(s)
    xo = rem(xh + c, 2)
    dest = [xo * NZ + rem(z + o, NZ) for o in off]
    source = [xo * NZ + rem(z + NZ - o, NZ) for o in off]
    to_self = (s == 0) & (c == 0)
    sibling = m + 1 - 2 * c
    steps = [(dy, dx) for dy in (2, 1, 3, 0) for dx in (1, 0) if (dy, dx) != (0, 0)]

    def chip(dy, dx):
        ty, tx_ = rem(y + dy, 4), rem(xl + dx, 2)
        return rem(ty, 2) * 2 + tx_, ty // 2, ty * 4 + tx_ * 2 + c

    columns = pl.ds(pl.multiple_of(fh * half, 128), half)
    loads = [
        pltpu.make_async_copy(src, dst, ld_sem.at[i])
        for i, (src, dst) in enumerate(
            ((tok_hbm.at[:, columns], tok), (cot_hbm.at[:, columns], cot), (win_hbm, win.at[0]), (wout_hbm, wout.at[0])))
    ]
    barrier = pltpu.get_barrier_semaphore()

    def greet(e, dp):
        pl.semaphore_signal(barrier, inc=1, device_id={"expert": e, "dp": dp}, device_id_type=pl.DeviceIdType.MESH)

    for i in (4, 5, 6, 7):
        greet(m, dest[i])
        greet(m, source[i])
    for copy in loads:
        copy.start()
    for i in (2, 3, 0):
        greet(m, dest[i])
        greet(m, source[i])

    @pl.when(jnp.logical_not(to_self))
    def _():
        greet(m, dest[1])
        greet(m, source[1])

    for dy, dx in steps:
        greet(chip(dy, dx)[2], d)
    for k in (1, 3, 5, 7):
        greet(fh * 8 + rem(mine + k, 8), d)

    id0, id1 = ids_ref[0:1, :], ids_ref[1:2, :]
    g0, g1 = gate_ref[0:1, :], gate_ref[1:2, :]
    count = id0.shape[1]
    earlier = (iota((count, count), 0) < iota((count, count), 1)).astype(BF16)

    def slots(expert, slot):
        one0, one1 = id0 == expert, id1 == expert
        one = one0 | one1
        before = jnp.dot(one.astype(F32).astype(BF16), earlier, preferred_element_type=F32)
        taken = one & (before.astype(jnp.int32) == slot)
        return taken, one0

    r = iota((128, 1), 0)
    ri, rq, rs = r // 16, rem(r // 4, 4), rem(r, 4)
    expert = jnp.zeros_like(r)
    for i in range(8):
        expert = jnp.where(ri == i, dest[i], expert)
    taken, one0 = slots(expert, rs)
    gate = jnp.sum(jnp.where(taken, jnp.where(one0, g0, g1), 0.0), axis=1, keepdims=True)
    picks = [(taken & (rq == q)).astype(F32).astype(BF16) for q in range(4)]

    def fill(stream, ref, scale):
        total = None
        for q in range(4):
            part = jnp.dot(picks[q], ref[:, q * piece:(q + 1) * piece], preferred_element_type=F32)
            total = part if total is None else total + part
        if scale is not None:
            total = total * scale
        tx[stream] = total.astype(BF16)

    loads[0].wait()
    fill(0, tok, None)
    loads[1].wait()
    fill(1, cot, gate)
    pl.semaphore_wait(barrier, 16 + 7 + 4 - 2 * to_self.astype(jnp.int32))

    waits, guarded = [], []

    def remote(src, dst, send, recv, e=None, dp=None):
        return pltpu.make_async_remote_copy(
            src_ref=src, dst_ref=dst, send_sem=send, recv_sem=recv,
            device_id={"expert": m if e is None else e, "dp": d if dp is None else dp},
            device_id_type=pl.DeviceIdType.MESH,
        )

    def go(copy):
        copy.start()
        waits.append(copy)
        return copy

    def exchange(src, dst, send, recv, dp, is_self):
        copy = remote(src, dst, send, recv, dp=dp)
        if not is_self:
            return go(copy)

        @pl.when(jnp.logical_not(to_self))
        def _():
            copy.start()

        @pl.when(to_self)
        def _():
            pltpu.make_async_copy(src, dst, recv).start()

        guarded.append(copy)
        return copy

    def block(ref, row, size=16):
        return ref.at[pl.ds(row if isinstance(row, int) else pl.multiple_of(row, 16), size)]

    b_copies = {}

    def send_b(way, order):
        for stream in range(2):
            for i in order:
                b_copies[stream, i] = exchange(
                    block(tx.at[stream], i * 16), block(packed.at[stream, way, fh], s * 64 + (i % 4) * 16),
                    b_s.at[stream, i], b_r.at[stream, i], dest[i], i == 1)

    send_b(1, (4, 5, 6, 7))

    weights = []
    for i, ref in enumerate((win, wout)):
        loads[2 + i].wait()
        weights.append(go(remote(ref.at[0], ref.at[1], w_s.at[i], w_r.at[i], e=sibling)))

    def matrix(n, same):
        return same(iota((n, n), 0), iota((n, n), 1)).astype(F32).astype(BF16)

    spread = matrix(256, lambda t, u: (t // 64 == rem(u // 4, 4)) & (rem(t // 4, 16) == u // 16) & (rem(t, 4) == rem(u, 4)))
    swap = matrix(64, lambda t, u: (t // 16 == rem(u // 4, 4)) & (rem(t // 4, 4) == u // 16) & (rem(t, 4) == rem(u, 4)))

    ar = iota((256, 1), 0)
    at, ai, asl = ar // 32, rem(ar // 4, 8), rem(ar, 4)
    aoff = jnp.zeros_like(ar)
    for i, o in enumerate(offsets(at // 2)):
        aoff = jnp.where(ai == i, o, aoff)
    all_taken, _ = slots(rem(xh + rem(at, 2), 2) * NZ + rem(z + aoff, NZ), asl)
    dall[...] = all_taken.astype(F32).astype(BF16)

    send_b(0, (2, 3, 0, 1))

    for way in range(2):
        for stream in range(2):
            for i in range(4 * way, 4 * way + 4):
                b_copies[stream, i].wait_recv()
            ref = block(packed.at[stream, way, fh], s * 64, 64)
            for k, step in enumerate(steps):
                go(remote(ref, ref, ag_s.at[stream, way, k], ag_r.at[stream, way, fh, s], e=chip(*step)[2]))

    def unpack(stream, way, target):
        for step in reversed(steps):
            ts_, tf, _ = chip(*step)
            ref = block(packed.at[stream, way, tf], ts_ * 64, 64)
            remote(ref, ref, ag_s.at[stream, way, 0], ag_r.at[stream, way, tf, ts_], e=sibling).wait_recv()
        for f in range(2):
            got = jnp.dot(spread, packed[stream, way, f], preferred_element_type=F32).astype(BF16)
            for q in range(4):
                cols = slice(f * half + q * piece, f * half + (q + 1) * piece)
                target[way * 64:(way + 1) * 64, cols] = got[q * 64:(q + 1) * 64]

    chunk = half // 2
    e_copies = []

    def send_e(way):
        row = []
        for k, step in enumerate(steps):
            ts_, tf, e = chip(*step)
            row.append(go(remote(
                block(es.at[way, tf], ts_ * 16), er.at[way, k], e_ss.at[way, k], e_rs.at[way, k], e=e)))
        e_copies.append(row)

    for way in range(2):
        rows = slice(way * 64, (way + 1) * 64)
        unpack(0, way, x_ref)
        if way == 0:
            weights[0].wait_recv()
        slopes = []
        for i in range(2):
            preact = None
            for k in range(4):
                cols = slice(k * chunk, (k + 1) * chunk)
                part = jnp.dot(x_ref[rows, cols], win[i, cols, :], preferred_element_type=F32)
                preact = part if preact is None else preact + part
            square = preact * preact
            th = jnp.tanh(K0 * preact * (1.0 + K1 * square))
            hid[i, rows, :] = (0.5 * preact * (1.0 + th)).astype(BF16)
            slopes.append(0.5 * (1.0 + th) + 0.5 * preact * (1.0 - th * th) * (K0 * (1.0 + 3.0 * K1 * square)))
        unpack(1, way, g_ref)
        if way == 0:
            weights[1].wait_recv()
        else:
            send_e(0)
        grads = []
        for i in range(2):
            post = None
            for k in range(4):
                cols = slice(k * chunk, (k + 1) * chunk)
                part = lax.dot_general(g_ref[rows, cols], wout[i, :, cols], NT, preferred_element_type=F32)
                post = part if post is None else post + part
            grads.append((post * slopes[i]).astype(BF16))
        for k in range(4):
            cols = slice(k * chunk, (k + 1) * chunk)
            part = lax.dot_general(grads[0], win[0, cols, :], NT, preferred_element_type=F32)
            part = part + lax.dot_general(grads[1], win[1, cols, :], NT, preferred_element_type=F32)
            here = slice((k % 2) * chunk, (k % 2 + 1) * chunk)
            q_ref[way, k // 2, :, here] = part
            es[way, k // 2, :, here] = part.astype(BF16)
        if way == 1:
            send_e(1)

    g_copy = go(remote(g_ref, g_sib, g_ss, g_rs, e=sibling))
    hid_copy = go(remote(hid.at[1], hid_sib, h_ss, h_rs, e=sibling))

    f_copies = []
    for way in range(2):
        total = q_ref[way, fh, pl.ds(pl.multiple_of(s * 16, 16), 16), :]
        for k in reversed(range(len(steps))):
            e_copies[way][k].wait_recv()
            total = total + er[way, k].astype(F32)
        total = total.astype(BF16)
        stacked = jnp.concatenate([total[:, q * piece:(q + 1) * piece] for q in range(4)], axis=0)
        fs[way] = jnp.dot(swap, stacked, preferred_element_type=F32).astype(BF16)
        f_copies.append([
            exchange(block(fs.at[way], j * 16), block(fr.at[way], j * 16), f_ss.at[way, j], f_rs.at[way, j],
                     source[4 * way + j], way == 0 and j == 1)
            for j in range(4)
        ])

    hid_copy.wait_recv()
    turned = jnp.concatenate([hid[0].astype(F32).T, hid_sib[...].astype(F32).T], axis=1).astype(BF16)
    g_copy.wait_recv()
    for k in range(4):
        cols = slice(k * chunk, (k + 1) * chunk)
        both = jnp.concatenate([g_ref[:, cols], g_sib[:, cols]], axis=0)
        wog[:, cols] = jnp.dot(turned, both, preferred_element_type=F32).astype(BF16)

    t_copies = []
    for way in range(2):
        for copy in f_copies[way]:
            copy.wait_recv()
        got = jnp.dot(swap, fr[way], preferred_element_type=F32).astype(BF16)
        for k in range(8):
            ts[way, k] = got[(k // 2) * 16:(k // 2 + 1) * 16, (k % 2) * 128:(k % 2 + 1) * 128]
        for k in range(1, 8):
            there = rem(mine + k, 8)
            t_copies.append(go(remote(
                ts.at[way, there], block(tr, mine * 32 + way * 16), t_ss.at[way, k], t_rs.at[way, k], e=fh * 8 + there)))
        tr[pl.ds(pl.multiple_of(mine * 32 + way * 16, 16), 16), :] = ts[way, mine]

    for copy in t_copies:
        copy.wait_recv()
    out_ref[...] = lax.dot_general(dall[...], tr[...], TN, preferred_element_type=F32).astype(BF16)

    for copy in waits:
        copy.wait_send()

    @pl.when(jnp.logical_not(to_self))
    def _():
        for copy in guarded:
            copy.wait_send()


def shards(tokens, cotangent, gate_values, expert_ids, weight_in, weight_out):
    count, width = tokens.shape
    hidden = weight_in.shape[2]
    dma = pltpu.SemaphoreType.DMA
    half = width // 2
    vmem = pl.BlockSpec(memory_space=pltpu.VMEM)
    hbm = pl.BlockSpec(memory_space=pltpu.HBM)
    out, grad = pl.pallas_call(
        kernel,
        out_shape=(
            pltpu.VMEM((count, width // PLANE), BF16),
            pltpu.VMEM((hidden, width), BF16),
        ),
        in_specs=[hbm, hbm, vmem, vmem, hbm, hbm],
        out_specs=(vmem, vmem),
        scratch_shapes=[
            pltpu.VMEM((count, half), BF16),
            pltpu.VMEM((count, half), BF16),
            pltpu.VMEM((2, width, hidden), BF16),
            pltpu.VMEM((2, hidden, width), BF16),
            pltpu.VMEM((2, 128, half // 4), BF16),
            pltpu.VMEM((2, 2, 2, 256, half // 4), BF16),
            pltpu.VMEM((128, width), BF16),
            pltpu.VMEM((128, width), BF16),
            pltpu.VMEM((128, width), BF16),
            pltpu.VMEM((2, 128, hidden), BF16),
            pltpu.VMEM((128, hidden), BF16),
            pltpu.VMEM((2, 2, 64, half), BF16),
            pltpu.VMEM((2, 7, 16, half), BF16),
            pltpu.VMEM((2, 2, 64, half), F32),
            pltpu.VMEM((2, 64, half // 4), BF16),
            pltpu.VMEM((2, 64, half // 4), BF16),
            pltpu.VMEM((2, 8, 16, width // PLANE), BF16),
            pltpu.VMEM((256, width // PLANE), BF16),
            pltpu.VMEM((256, count), BF16),
            dma((4,)),
            dma((2, 8)), dma((2, 8)),
            dma((2,)), dma((2,)),
            dma((2, 2, 7)), dma((2, 2, 2, 4)),
            dma, dma,
            dma, dma,
            dma((2, 7)), dma((2, 7)),
            dma((2, 4)), dma((2, 4)),
            dma((2, 8)), dma((2, 8)),
        ],
        compiler_params=pltpu.CompilerParams(
            collective_id=0, has_side_effects=True, vmem_limit_bytes=58 * 1024 * 1024
        ),
    )(tokens, cotangent, expert_ids.T, gate_values.T, weight_in[0], weight_out[0])
    return out, grad[None]


def solution(mesh):
    placed = (
        P("dp", None),
        P("dp", None),
        P("dp", None),
        P("dp", None),
        P("dp", None, "expert"),
        P("dp", "expert", None),
    )
    return jax.shard_map(
        shards,
        mesh=mesh,
        in_specs=placed,
        out_specs=(P("dp", "expert"), P("dp", "expert", None)),
        check_vma=False,
    )
```
